32 devices in a mesh: band: 4 (over y, x), pair: 8 (over z, core).
Axes of the slice: x: 2, y: 2, z: 4, core: 2. Of those that a mesh axis runs over, the one named last changes fastest.
Arguments:
- traces: float32 [16, 8192, 1024], P('band', 'pair'), may hold values from -300 to 300
- pair_list: int32 [16, 2], replicated, may hold values from 0 to 63, as said below
- pair_owner: int32 [16], replicated, may hold values from 0 to 15, as said below
Outputs:
- cross_spectra: bfloat16 [16, 2, 128, 128, 512], P('pair', None, None, None, 'band')
The draws below stay inside these ranges and needn't reach their ends.
Inputs may be any that keep to these rules, and one draw needn't show every extreme that they name: `pair_list`: each row (i, j) has 8 <= j - i <= 24; index p of pair holds blocks p * 64 / 8 up to (p + 1) * 64 / 8 - 1, and the 4 blocks named by the rows of one owner (pair_owner // 2) all lie on different indices of pair. `pair_owner`: every slot is named by exactly 1 row.
All inputs are finite; a program needn't handle non-finite values.
Results may differ from the reference program's by a relative error of at most 0.0057.
Values may be sent and summed in bfloat16 or wider, within the bound.
A program may use at most 320 MiB of HBM per device.

```python
import jax
import jax.numpy as jnp
from jax import lax

S = 1024
F = 512
SUB = 64
CHANNELS = 8192
BLOCK = 128
BLOCKS = 64
WINDOWS = 16
SLOTS = 2
OWNER_SLOTS = 16
PER_SLOT = 1


def pair_draw(key):
    inner = jax.random.fold_in(key, 7)
    key_start, key_perm, key_left, key_right, key_shuffle = jax.random.split(inner, 5)
    owner_count = OWNER_SLOTS // SLOTS
    quarter = owner_count // 4
    per_owner_slot = quarter // SLOTS
    per_device = BLOCKS // owner_count
    starts = jax.random.randint(key_start, (owner_count,), 0, owner_count // 2 + 1)
    starts = starts.at[0].set(owner_count // 2).at[1].set(0)
    owner_ids = jnp.arange(owner_count)
    orders = jax.vmap(lambda owner: jax.random.permutation(jax.random.fold_in(key_perm, owner), quarter))(owner_ids)
    left_device = starts[:, None] + orders
    right_device = left_device + quarter
    left_offset = jax.random.randint(key_left, (owner_count, quarter), 0, per_device)
    right_offset = jax.random.randint(key_right, (owner_count, quarter), 0, per_device)
    left_offset = left_offset.at[1].set(0)
    right_offset = right_offset.at[0].set(per_device - 1)
    first_block = left_device * per_device + left_offset
    second_block = right_device * per_device + right_offset
    slot_rows = owner_ids[:, None] * SLOTS + jnp.arange(quarter)[None, :] // per_owner_slot
    pair_rows = jnp.stack([first_block.reshape(-1), second_block.reshape(-1)], axis=1)
    shuffle = jax.random.permutation(key_shuffle, pair_rows.shape[0])
    return (pair_rows[shuffle].astype(jnp.int32), slot_rows.reshape(-1)[shuffle].astype(jnp.int32))


def draw_pair_list(key, part):
    return pair_draw(key)[0]


def draw_pair_owner(key, part):
    return pair_draw(key)[1]


def draw_traces(key, part):
    key_noise, key_channel, key_window = jax.random.split(key, 3)
    shape_all = (WINDOWS, CHANNELS, S)
    noise = jax.random.truncated_normal(key_noise, -6.0, 6.0, shape_all, jnp.float32)
    top_gain = 10.0
    channel_gain = jnp.exp(jax.random.uniform(key_channel, (1, CHANNELS, 1), jnp.float32, 0.0, jnp.log(top_gain)))
    window_gain = jnp.exp(jax.random.uniform(key_window, (WINDOWS, 1, 1), jnp.float32, 0.0, jnp.log(4.0)))
    return noise * channel_gain * window_gain


def setup_inputs(seed: int = 0) -> dict:
    key_list = jax.random.split(jax.random.key(seed), 4)
    traces = draw_traces(jax.random.fold_in(key_list[3], 71), 0)
    pair_list = draw_pair_list(jax.random.fold_in(key_list[3], 71), 0)
    pair_owner = draw_pair_owner(jax.random.fold_in(key_list[3], 71), 0)
    return {"traces": traces, "pair_list": pair_list, "pair_owner": pair_owner}


whiten_eps = 1e-05

def whiten(traces):
    spectra = jnp.fft.rfft(traces, axis=-1)[..., :F]
    real_part = jnp.real(spectra)
    imag_part = jnp.imag(spectra)
    shape_sub = traces.shape[:-1] + (F // SUB, SUB)
    real_band = real_part.reshape(shape_sub)
    imag_band = imag_part.reshape(shape_sub)
    band_power = lax.optimization_barrier(jnp.mean(real_band * real_band + imag_band * imag_band, axis=-1, keepdims=True))
    factor = lax.rsqrt(band_power + whiten_eps)
    stacked = jnp.stack([real_band * factor, imag_band * factor], axis=2)
    return stacked.reshape(traces.shape[:-1] + (2, F)).astype(jnp.bfloat16)

def reference(traces, pair_list, pair_owner):
    whitened = whiten(traces)
    order = jnp.argsort(pair_owner, stable=True)
    grouped = pair_list[order].reshape(OWNER_SLOTS, PER_SLOT, 2)

    def one_pair(blocks):
        start_left = (blocks[0] * BLOCK).astype(jnp.int32)
        start_right = (blocks[1] * BLOCK).astype(jnp.int32)
        left_rows = lax.dynamic_slice_in_dim(whitened, start_left, BLOCK, axis=1).astype(jnp.float32)
        right_rows = lax.dynamic_slice_in_dim(whitened, start_right, BLOCK, axis=1).astype(jnp.float32)
        rotated = jnp.stack([left_rows[:, :, 1], -left_rows[:, :, 0]], axis=2)
        paired = jnp.stack([left_rows, rotated], axis=1)
        return jnp.einsum('wcakf,wbkf->cabf', paired, right_rows)

    def one_slot(slot_pairs):

        def add_pair(step, total):
            return total + one_pair(slot_pairs[step])
        start = jnp.zeros((2, BLOCK, BLOCK, F), jnp.float32)
        return lax.fori_loop(0, PER_SLOT, add_pair, start).astype(jnp.bfloat16)
    return lax.map(one_slot, grouped)
```

```python
import functools

import jax
import jax.numpy as jnp
import ml_dtypes
import numpy as np
from jax import lax
from jax.experimental import pallas as pl
from jax.experimental.pallas import tpu as pltpu
from jax.sharding import PartitionSpec as P

SUB = 64
BLOCK = 128
SLOTS = 2
whiten_eps = 1e-05
MESH = pl.DeviceIdType.MESH


def dft_tables(samples, bands):
    half = samples // 2
    n = np.arange(half)
    wide = half // bands // 2
    tables = []
    for parity in range(2):
        bins = 2 * np.arange(bands * wide).reshape(bands, wide) + parity
        phase = (bins[:, :, None] * n % samples) * (2.0 * np.pi / samples)
        table = np.stack([np.cos(phase), -np.sin(phase)], axis=1).reshape(half, half)
        high = table.astype(np.float32).astype(ml_dtypes.bfloat16)
        low = (table - high.astype(np.float64)).astype(np.float32).astype(ml_dtypes.bfloat16)
        tables.append(np.concatenate([high, low, high], axis=1))
    return np.stack(tables)


def whiten_kernel(bands, index_ref, wanted_ref, table_ref, traces_ref, out_ref):
    owner = pl.program_id(0)
    windows, block, samples = traces_ref.shape
    half = samples // 2
    wide = half // bands // 2
    part = SUB // 2

    @pl.when(wanted_ref[owner] > 0)
    def _():
        x = traces_ref[...].reshape(windows * block, samples)
        spectra = []
        for parity in range(2):
            first, second = x[:, :half], x[:, half:]
            folded = first + second if parity == 0 else first - second
            high = folded.astype(jnp.bfloat16)
            low = (folded - high.astype(jnp.float32)).astype(jnp.bfloat16)
            operand = jnp.concatenate([high, high, low], axis=1)
            spectra.append(
                lax.dot_general(
                    table_ref[parity],
                    operand,
                    (((1,), (1,)), ((), ())),
                    preferred_element_type=jnp.float32,
                )
            )
        for band in range(bands):
            for sub in range(wide // part):
                rows = [
                    [
                        spectra[parity][(band * 2 + k) * wide + sub * part :][:part]
                        for k in range(2)
                    ]
                    for parity in range(2)
                ]
                power = sum(r * r for pair in rows for r in pair)
                mean = jnp.sum(power, axis=0, keepdims=True) * (1.0 / SUB)
                factor = lax.rsqrt(mean + whiten_eps)
                for parity in range(2):
                    for k in range(2):
                        white = (rows[parity][k] * factor).astype(jnp.bfloat16)
                        at = parity * wide + sub * part
                        for w in range(windows):
                            out_ref[band, 0, w, k, at : at + part, :] = white[
                                :, w * block : (w + 1) * block
                            ]

    @pl.when(wanted_ref[owner] == 0)
    def _():
        out_ref[...] = jnp.zeros_like(out_ref)


def whiten(traces, send_index, wanted, bands):
    win_local, _, samples = traces.shape
    owners = send_index.shape[0]
    half = samples // 2
    group = 2
    table = jnp.asarray(dft_tables(samples, bands))
    return pl.pallas_call(
        functools.partial(whiten_kernel, bands),
        grid_spec=pltpu.PrefetchScalarGridSpec(
            num_scalar_prefetch=2,
            grid=(owners, win_local // group),
            in_specs=[
                pl.BlockSpec(table.shape, lambda o, w, index, wanted: (0, 0, 0)),
                pl.BlockSpec(
                    (group, BLOCK, samples), lambda o, w, index, wanted: (w, index[o], 0)
                ),
            ],
            out_specs=pl.BlockSpec(
                (bands, 1, group, 2, half // bands, BLOCK),
                lambda o, w, index, wanted: (0, o, w, 0, 0, 0),
            ),
        ),
        out_shape=jax.ShapeDtypeStruct(
            (bands, owners, win_local, 2, half // bands, BLOCK), jnp.bfloat16
        ),
        compiler_params=pltpu.CompilerParams(vmem_limit_bytes=48 * 2**20),
        name="whiten",
    )(send_index, wanted, table, traces)


def exchange_kernel(bands, owners, send_ref, recv_ref, local_sem, send_sem, recv_sem):
    count = bands * owners
    my_band, my_pair = lax.axis_index("band"), lax.axis_index("pair")
    me = my_band * owners + my_pair
    barrier = pltpu.get_barrier_semaphore()

    def place(step):
        flat = lax.rem(me + step, count)
        return flat // owners, lax.rem(flat, owners)

    def greet(step, carry):
        pl.semaphore_signal(barrier, inc=1, device_id=place(step), device_id_type=MESH)
        return carry

    lax.fori_loop(1, count, greet, 0)
    own = pltpu.make_async_copy(
        send_ref.at[my_band, my_pair], recv_ref.at[my_band, my_pair], local_sem
    )
    own.start()
    pl.semaphore_wait(barrier, count - 1)

    def copy(step):
        band, pair = place(step)
        return pltpu.make_async_remote_copy(
            src_ref=send_ref.at[band, pair],
            dst_ref=recv_ref.at[my_band, my_pair],
            send_sem=send_sem.at[step],
            recv_sem=recv_sem.at[step],
            device_id=(band, pair),
            device_id_type=MESH,
        )

    def start(step, carry):
        copy(step).start()
        return carry

    lax.fori_loop(1, count, start, 0)
    own.wait()

    def finish(step, carry):
        copy(step).wait()
        return carry

    lax.fori_loop(1, count, finish, 0)


def exchange(outgoing):
    bands, owners = outgoing.shape[:2]
    return pl.pallas_call(
        functools.partial(exchange_kernel, bands, owners),
        out_shape=jax.ShapeDtypeStruct(outgoing.shape, outgoing.dtype),
        in_specs=[pl.BlockSpec(memory_space=pl.ANY)],
        out_specs=pl.BlockSpec(memory_space=pl.ANY),
        scratch_shapes=[
            pltpu.SemaphoreType.DMA,
            pltpu.SemaphoreType.DMA((bands * owners,)),
            pltpu.SemaphoreType.DMA((bands * owners,)),
        ],
        compiler_params=pltpu.CompilerParams(collective_id=0, has_side_effects=True),
        name="exchange",
    )(outgoing)


def stack_kernel(first_ref, second_ref, left_ref, right_ref, out_ref, left32, right32, total):
    rank = pl.program_id(1)
    groups, _, win_local, _, wide, block = left_ref.shape
    windows = groups * win_local

    for g in range(groups):
        for w in range(win_local):
            for k in range(2):
                at = ((g * win_local + w) * 2 + k) * wide
                left32[at : at + wide, :] = left_ref[g, 0, w, k].astype(jnp.float32)
                right32[at : at + wide, :] = right_ref[g, 0, w, k].astype(jnp.float32)

    def read(ref, row):
        parts = [
            ref[pl.ds(k * wide + row, windows, stride=2 * wide), :] for k in range(2)
        ]
        return [p.astype(jnp.bfloat16) for p in parts]

    def correlate(accumulate):
        def one(m, carry):
            for parity in range(2):
                row = parity * (wide // 2) + m
                bin_ = 2 * m + parity
                lre, lim = read(left32, row)
                rre, rim = read(right32, row)
                lhs = jnp.concatenate([lre, lim], axis=0)
                rhs = jnp.concatenate(
                    [
                        jnp.concatenate([rre, rim], axis=0),
                        jnp.concatenate([-rim, rre], axis=0),
                    ],
                    axis=1,
                )
                product = lax.dot_general(
                    lhs, rhs, (((0,), (0,)), ((), ())), preferred_element_type=jnp.float32
                )
                for c in range(2):
                    rows = pl.ds(c * block * wide + bin_, block, stride=wide)
                    value = product[:, c * block : (c + 1) * block]
                    total[rows, :] = total[rows, :] + value if accumulate else value
            return carry

        lax.fori_loop(0, wide // 2, one, 0, unroll=2)

    if first_ref.shape[1] == 1:
        correlate(False)
    else:
        pl.when(rank == 0)(lambda: correlate(False))
        pl.when(rank > 0)(lambda: correlate(True))

    @pl.when(rank == first_ref.shape[1] - 1)
    def _():
        def turn(a, carry):
            for c in range(2):
                start = pl.multiple_of((c * block + a) * wide, wide)
                out_ref[0, c, a] = total[pl.ds(start, wide), :].T.astype(jnp.bfloat16)
            return carry

        lax.fori_loop(0, block, turn, 0, unroll=4)


def stack_pairs(received, source_first, source_second):
    groups, _, win_local, _, wide, block = received.shape
    slots, per_slot = source_first.shape
    piece = (groups, 1, win_local, 2, wide, block)
    rows = groups * win_local * 2 * wide
    return pl.pallas_call(
        stack_kernel,
        grid_spec=pltpu.PrefetchScalarGridSpec(
            num_scalar_prefetch=2,
            grid=(slots, per_slot),
            in_specs=[
                pl.BlockSpec(piece, lambda s, r, first, second: (0, first[s, r], 0, 0, 0, 0)),
                pl.BlockSpec(piece, lambda s, r, first, second: (0, second[s, r], 0, 0, 0, 0)),
            ],
            out_specs=pl.BlockSpec(
                (1, 2, block, block, wide), lambda s, r, first, second: (s, 0, 0, 0, 0)
            ),
            scratch_shapes=[
                pltpu.VMEM((rows, block), jnp.float32),
                pltpu.VMEM((rows, block), jnp.float32),
                pltpu.VMEM((2 * block * wide, block), jnp.float32),
            ],
        ),
        out_shape=jax.ShapeDtypeStruct((slots, 2, block, block, wide), jnp.bfloat16),
        compiler_params=pltpu.CompilerParams(vmem_limit_bytes=56 * 2**20),
        name="stack_pairs",
    )(source_first, source_second, received, received)


def shards(traces, pair_list, pair_owner):
    bands = lax.axis_size("band")
    owners = lax.axis_size("pair")
    per_device = traces.shape[1] // BLOCK
    pairs = pair_list.shape[0]
    per_slot = pairs // (owners * SLOTS)
    device_index = lax.axis_index("pair")
    named = pair_list // per_device
    owner_ids = jnp.arange(owners, dtype=jnp.int32)
    mine = (
        (pair_owner // SLOTS)[:, None, None] == owner_ids[None, :, None]
    ) & (named == device_index)[:, None, :]
    wanted = jnp.max(mine.astype(jnp.int32), axis=(0, 2))
    local = pair_list - device_index * per_device
    send_index = jnp.max(jnp.where(mine, local[:, None, :], 0), axis=(0, 2))
    order = jnp.arange(pairs, dtype=jnp.int32)
    earlier = (pair_owner[:, None] == pair_owner[None, :]) & (order[None, :] < order[:, None])
    rank = jnp.sum(earlier.astype(jnp.int32), axis=1)
    slot_ids = device_index * SLOTS + jnp.arange(SLOTS, dtype=jnp.int32)
    rank_ids = jnp.arange(per_slot, dtype=jnp.int32)
    selected = (pair_owner[:, None, None] == slot_ids[None, :, None]) & (
        rank[:, None, None] == rank_ids[None, None, :]
    )
    source_first = jnp.sum(jnp.where(selected, named[:, 0][:, None, None], 0), axis=0)
    source_second = jnp.sum(jnp.where(selected, named[:, 1][:, None, None], 0), axis=0)
    outgoing = whiten(traces, send_index, wanted, bands)
    received = exchange(outgoing)
    return stack_pairs(received, source_first, source_second)


def solution(mesh):
    placed = (P("band", "pair", None), P(), P())
    return jax.shard_map(
        shards,
        mesh=mesh,
        in_specs=placed,
        out_specs=P("pair", None, None, None, "band"),
        check_vma=False,
    )
```

```python
import functools

import jax
import jax.numpy as jnp
import ml_dtypes
import numpy as np
from jax import lax
from jax.experimental import pallas as pl
from jax.experimental.pallas import tpu as pltpu
from jax.sharding import PartitionSpec as P

SUB = 64
BLOCK = 128
SLOTS = 2
PAD = 8
whiten_eps = 1e-05
MESH = pl.DeviceIdType.MESH


def dft_tables(samples, bands):
    half = samples // 2
    n = np.arange(half)
    wide = half // bands // 2
    tables = []
    for parity in range(2):
        bins = 2 * np.arange(bands * wide).reshape(bands, wide) + parity
        phase = (bins[:, :, None] * n % samples) * (2.0 * np.pi / samples)
        table = np.stack([np.cos(phase), -np.sin(phase)], axis=1).reshape(half, half)
        high = table.astype(np.float32).astype(ml_dtypes.bfloat16)
        low = (table - high.astype(np.float64)).astype(np.float32).astype(ml_dtypes.bfloat16)
        tables.append(np.concatenate([high, low, high], axis=1))
    return np.stack(tables)


def wanted_block(owner, pair_ref, list_ref, owner_ref, per_device):
    start = pair_ref[0] * per_device
    index, found = jnp.int32(0), jnp.int32(0)
    for k in range(owner_ref.shape[0]):
        slot = owner_ref[k] - owner * SLOTS
        for side in range(2):
            local = list_ref[k * 2 + side] - start
            hit = (slot >= 0) & (slot < SLOTS) & (local >= 0) & (local < per_device)
            index = jnp.where(hit, local, index)
            found = jnp.where(hit, 1, found)
    return index, found


def source_of(slot, rank, side, pair_ref, list_ref, owner_ref, per_device):
    slot = pair_ref[0] * SLOTS + slot
    named, seen = jnp.int32(0), jnp.int32(0)
    for k in range(owner_ref.shape[0]):
        hit = owner_ref[k] == slot
        named = jnp.where(hit & (seen == rank), list_ref[k * 2 + side], named)
        seen = seen + jnp.where(hit, 1, 0)
    return named // per_device


def whiten_kernel(bands, per_device, pair_ref, list_ref, owner_ref, table_ref, traces_ref, out_ref):
    _, found = wanted_block(pl.program_id(0), pair_ref, list_ref, owner_ref, per_device)
    windows, block, samples = traces_ref.shape
    half = samples // 2
    wide = half // bands // 2
    part = SUB // 2

    @pl.when(found > 0)
    def _():
        x = traces_ref[...].reshape(windows * block, samples)
        spectra = []
        for parity in range(2):
            first, second = x[:, :half], x[:, half:]
            folded = first + second if parity == 0 else first - second
            high = folded.astype(jnp.bfloat16)
            low = (folded - high.astype(jnp.float32)).astype(jnp.bfloat16)
            operand = jnp.concatenate([high, high, low], axis=1)
            spectra.append(
                lax.dot_general(
                    table_ref[parity],
                    operand,
                    (((1,), (1,)), ((), ())),
                    preferred_element_type=jnp.float32,
                )
            )
        for band in range(bands):
            for sub in range(wide // part):
                rows = [
                    [
                        spectra[parity][(band * 2 + k) * wide + sub * part :][:part]
                        for k in range(2)
                    ]
                    for parity in range(2)
                ]
                power = sum(r * r for pair in rows for r in pair)
                mean = jnp.sum(power, axis=0, keepdims=True) * (1.0 / SUB)
                factor = lax.rsqrt(mean + whiten_eps)
                for parity in range(2):
                    for k in range(2):
                        white = (rows[parity][k] * factor).astype(jnp.bfloat16)
                        at = parity * wide + sub * part
                        for w in range(windows):
                            out_ref[band, 0, w, k, at : at + part, :] = white[
                                :, w * block : (w + 1) * block
                            ]

    @pl.when(found == 0)
    def _():
        out_ref[...] = jnp.zeros_like(out_ref)


def whiten(traces, pair, pair_list, pair_owner, bands, owners):
    win_local, channels, samples = traces.shape
    per_device = channels // BLOCK
    half = samples // 2
    group = 2
    table = jnp.asarray(dft_tables(samples, bands))
    return pl.pallas_call(
        functools.partial(whiten_kernel, bands, per_device),
        grid_spec=pltpu.PrefetchScalarGridSpec(
            num_scalar_prefetch=3,
            grid=(owners, win_local // group),
            in_specs=[
                pl.BlockSpec(table.shape, lambda o, w, *refs: (0, 0, 0)),
                pl.BlockSpec(
                    (group, BLOCK, samples),
                    lambda o, w, *refs: (w, wanted_block(o, *refs, per_device)[0], 0),
                ),
            ],
            out_specs=pl.BlockSpec(
                (bands, 1, group, 2, half // bands, BLOCK),
                lambda o, w, *refs: (0, o, w, 0, 0, 0),
            ),
        ),
        out_shape=jax.ShapeDtypeStruct(
            (bands, owners, win_local, 2, half // bands, BLOCK), jnp.bfloat16
        ),
        compiler_params=pltpu.CompilerParams(vmem_limit_bytes=48 * 2**20),
        name="whiten",
    )(pair, pair_list, pair_owner, table, traces)


def exchange_kernel(bands, owners, send_ref, recv_ref, local_sem, send_sem, recv_sem):
    count = bands * owners
    my_band, my_pair = lax.axis_index("band"), lax.axis_index("pair")
    barrier = pltpu.get_barrier_semaphore()

    def place(step):
        shift = lax.rem(step // bands * (owners // 2 + 1), owners)
        return lax.rem(my_band + lax.rem(step, bands), bands), lax.rem(my_pair + shift, owners)

    def greet(step, carry):
        pl.semaphore_signal(barrier, inc=1, device_id=place(step), device_id_type=MESH)
        return carry

    lax.fori_loop(1, count, greet, 0)
    own = pltpu.make_async_copy(
        send_ref.at[my_band, my_pair], recv_ref.at[my_band, my_pair], local_sem
    )
    own.start()
    pl.semaphore_wait(barrier, count - 1)

    def copy(step):
        band, pair = place(step)
        return pltpu.make_async_remote_copy(
            src_ref=send_ref.at[band, pair],
            dst_ref=recv_ref.at[my_band, my_pair],
            send_sem=send_sem.at[step],
            recv_sem=recv_sem.at[step],
            device_id=(band, pair),
            device_id_type=MESH,
        )

    def start(step, carry):
        copy(step).start()
        return carry

    lax.fori_loop(1, count, start, 0)
    own.wait()

    def finish(step, carry):
        copy(step).wait()
        return carry

    lax.fori_loop(1, count, finish, 0)


def exchange(outgoing):
    bands, owners = outgoing.shape[:2]
    return pl.pallas_call(
        functools.partial(exchange_kernel, bands, owners),
        out_shape=jax.ShapeDtypeStruct(outgoing.shape, outgoing.dtype),
        in_specs=[pl.BlockSpec(memory_space=pl.ANY)],
        out_specs=pl.BlockSpec(memory_space=pl.ANY),
        scratch_shapes=[
            pltpu.SemaphoreType.DMA,
            pltpu.SemaphoreType.DMA((bands * owners,)),
            pltpu.SemaphoreType.DMA((bands * owners,)),
        ],
        compiler_params=pltpu.CompilerParams(collective_id=0, has_side_effects=True),
        name="exchange",
    )(outgoing)


def stack_kernel(
    per_slot, pair_ref, list_ref, owner_ref, left_ref, right_ref, out_ref, left32, right32, total
):
    rank = pl.program_id(1)
    groups, _, win_local, _, wide, block = left_ref.shape
    windows = groups * win_local
    pitch = wide + PAD

    for g in range(groups):
        for w in range(win_local):
            for k in range(2):
                at = ((g * win_local + w) * 2 + k) * pitch
                left32[at : at + wide, :] = left_ref[g, 0, w, k].astype(jnp.float32)
                right32[at : at + wide, :] = right_ref[g, 0, w, k].astype(jnp.float32)

    def read(ref, row):
        parts = [
            ref[pl.ds(k * pitch + row, windows, stride=2 * pitch), :] for k in range(2)
        ]
        return [p.astype(jnp.bfloat16) for p in parts]

    def correlate(accumulate):
        def one(m, carry):
            for parity in range(2):
                row = parity * (wide // 2) + m
                bin_ = 2 * m + parity
                lre, lim = read(left32, row)
                rre, rim = read(right32, row)
                lhs = jnp.concatenate([lre, lim], axis=0)
                rhs = jnp.concatenate(
                    [
                        jnp.concatenate([rre, rim], axis=0),
                        jnp.concatenate([-rim, rre], axis=0),
                    ],
                    axis=1,
                )
                product = lax.dot_general(
                    lhs, rhs, (((0,), (0,)), ((), ())), preferred_element_type=jnp.float32
                )
                for c in range(2):
                    rows = pl.ds(c * block * pitch + bin_, block, stride=pitch)
                    value = product[:, c * block : (c + 1) * block]
                    total[rows, :] = total[rows, :] + value if accumulate else value
            return carry

        lax.fori_loop(0, wide // 2, one, 0, unroll=4)

    if per_slot == 1:
        correlate(False)
    else:
        pl.when(rank == 0)(lambda: correlate(False))
        pl.when(rank > 0)(lambda: correlate(True))

    @pl.when(rank == per_slot - 1)
    def _():
        def turn(a, carry):
            for c in range(2):
                start = pl.multiple_of((c * block + a) * pitch, 8)
                out_ref[0, c, a] = total[pl.ds(start, wide), :].T.astype(jnp.bfloat16)
            return carry

        lax.fori_loop(0, block, turn, 0, unroll=8)


def stack_pairs(received, pair, pair_list, pair_owner, per_device):
    groups, owners, win_local, _, wide, block = received.shape
    slots, per_slot = SLOTS, pair_owner.shape[0] // (owners * SLOTS)
    piece = (groups, 1, win_local, 2, wide, block)
    rows = groups * win_local * 2 * (wide + PAD)
    return pl.pallas_call(
        functools.partial(stack_kernel, per_slot),
        grid_spec=pltpu.PrefetchScalarGridSpec(
            num_scalar_prefetch=3,
            grid=(slots, per_slot),
            in_specs=[
                pl.BlockSpec(
                    piece,
                    lambda s, r, *refs: (0, source_of(s, r, 0, *refs, per_device), 0, 0, 0, 0),
                ),
                pl.BlockSpec(
                    piece,
                    lambda s, r, *refs: (0, source_of(s, r, 1, *refs, per_device), 0, 0, 0, 0),
                ),
            ],
            out_specs=pl.BlockSpec(
                (1, 2, block, block, wide), lambda s, r, *refs: (s, 0, 0, 0, 0)
            ),
            scratch_shapes=[
                pltpu.VMEM((rows, block), jnp.float32),
                pltpu.VMEM((rows, block), jnp.float32),
                pltpu.VMEM((2 * block * (wide + PAD), block), jnp.float32),
            ],
        ),
        out_shape=jax.ShapeDtypeStruct((slots, 2, block, block, wide), jnp.bfloat16),
        compiler_params=pltpu.CompilerParams(vmem_limit_bytes=56 * 2**20),
        name="stack_pairs",
    )(pair, pair_list, pair_owner, received, received)


def shards(traces, pair_list, pair_owner):
    bands = lax.axis_size("band")
    owners = lax.axis_size("pair")
    per_device = traces.shape[1] // BLOCK
    pair = lax.axis_index("pair").astype(jnp.int32).reshape(1)
    flat_list = pair_list.reshape(-1)
    outgoing = whiten(traces, pair, flat_list, pair_owner, bands, owners)
    received = exchange(outgoing)
    return stack_pairs(received, pair, flat_list, pair_owner, per_device)


def solution(mesh):
    placed = (P("band", "pair", None), P(), P())
    return jax.shard_map(
        shards,
        mesh=mesh,
        in_specs=placed,
        out_specs=P("pair", None, None, None, "band"),
        check_vma=False,
    )
```
